32 devices in a mesh: row: 4 (over y, core), col: 8 (over z, x).
Axes of the slice: x: 2, y: 2, z: 4, core: 2. Of those that a mesh axis runs over, the one named last changes fastest.
Arguments:
- amps: bfloat16 [512, 64, 256], P('row', 'col'), may hold values from -6 to 6
- ints: bfloat16 [2048, 256, 256], P(('row', 'col')), may hold values from -0.046875 to 0.046875
- task_cd: int32 [2048], P(('row', 'col')), may hold values from 0 to 7, as said below
- task_ab: int32 [2048], P(('row', 'col')), may hold values from 0 to 7
- task_count: int32 [32], P(('row', 'col')), may hold values from 8 to 64, as said below
Outputs:
- residual: bfloat16 [512, 32, 256], P('col', 'row')
The draws below stay inside these ranges and needn't reach their ends.
Inputs may be any that keep to these rules, and one draw needn't show every extreme that they name: On each device the slots name distinct (task_cd, task_ab) pairs. The live slots of a device are its first task_count ones; some device has all 64 slots live in every draw.
All inputs are finite; a program needn't handle non-finite values.
Results may differ from the reference program's by a relative error of at most 0.001.
Values may be sent and summed in bfloat16 or wider, within the bound.
No kernel may reach another device: no remote copies, remote signals or barrier semaphores. Data moves between devices by JAX's collectives and lax.ppermute only.
A program may use at most 128 MiB of HBM per device.

```python
import jax
import jax.numpy as jnp
from jax import lax

TILE_PAIRS = 256
CD_COL = 8
PAIR_TILES_ROW = 8
DEVICE_SLOTS = 64
OCC = 512
NCD = 64
TOTAL_SLOTS = 2048
N_ROW = 4
N_COL = 8


def task_tables(key):
    base = jax.random.fold_in(key, 7131)
    groups = N_ROW * N_COL
    keys = jax.random.split(jax.random.fold_in(base, 1), groups)

    def pick(one_key):
        return jax.random.permutation(one_key, CD_COL * PAIR_TILES_ROW)[:DEVICE_SLOTS].astype(jnp.int32)
    pairs = jax.vmap(pick)(keys).reshape(groups * DEVICE_SLOTS)
    shifts = jax.random.randint(jax.random.fold_in(base, 2), (groups,), 0, 4).astype(jnp.int32)
    counts = jnp.right_shift(jnp.full((groups,), DEVICE_SLOTS, jnp.int32), shifts)
    counts = jnp.maximum(counts, max(DEVICE_SLOTS // 8, 1))
    heavy = jax.random.randint(jax.random.fold_in(base, 3), (), 0, groups).astype(jnp.int32)
    counts = jnp.where(jnp.arange(groups, dtype=jnp.int32) == heavy, DEVICE_SLOTS, counts).astype(jnp.int32)
    return (pairs // PAIR_TILES_ROW, pairs % PAIR_TILES_ROW, counts)


def draw_task_cd(key, part):
    return task_tables(key)[0]


def draw_task_ab(key, part):
    return task_tables(key)[1]


def draw_task_count(key, part):
    return task_tables(key)[2]


def levels(stream_key, dims, pieces, low, high):
    loudness, own = 1.0, jax.random.fold_in(stream_key, 6)
    for axis_at, blocks in pieces:
        heights = jnp.exp(jax.random.uniform(jax.random.fold_in(own, axis_at), (blocks,), jnp.float32, low / len(pieces), high / len(pieces)))
        loudness = loudness * jnp.repeat(heights, dims[axis_at] // blocks).reshape([-1 if axis == axis_at else 1 for axis in range(len(dims))])
    return loudness


def normal_values(key, extent, width, limit, shards=(), kind=jnp.bfloat16):
    result = width * jax.random.normal(key, extent, jnp.float32)
    if shards:
        result = result * levels(key, extent, shards, -0.22, 0.18)
    return jnp.clip(result, -limit, limit).astype(kind)


def setup_inputs(seed: int = 0) -> dict:
    key_list = jax.random.split(jax.random.key(seed), 6)
    return {
        "amps": normal_values(key_list[0], (OCC, NCD, TILE_PAIRS), 1.0, 6.0, ((0, 4), (1, 8))),
        "ints": normal_values(key_list[1], (TOTAL_SLOTS, TILE_PAIRS, TILE_PAIRS), (TILE_PAIRS * N_COL * DEVICE_SLOTS // PAIR_TILES_ROW) ** -0.5, 0.046875, ((0, 32),)),
        "task_cd": draw_task_cd(jax.random.fold_in(key_list[5], 71), 0),
        "task_ab": draw_task_ab(jax.random.fold_in(key_list[5], 71), 0),
        "task_count": draw_task_count(jax.random.fold_in(key_list[5], 71), 0),
    }


def reference(amps, ints, task_cd, task_ab, task_count):
    occ = amps.shape[0]
    ints_dev = ints.reshape(N_ROW, N_COL, DEVICE_SLOTS, TILE_PAIRS, TILE_PAIRS)
    device_cd_tiles = task_cd.reshape(N_ROW, N_COL, DEVICE_SLOTS)
    ab_dev = task_ab.reshape(N_ROW, N_COL, DEVICE_SLOTS)
    count_dev = task_count.reshape(N_ROW, N_COL)

    def one_row(row_index):
        def one_col(total, col_index):
            def one_slot(slot, acc):
                def add_term(inner):
                    cd_tile = (col_index * CD_COL + device_cd_tiles[row_index, col_index, slot]).astype(jnp.int32)
                    tile_amps = lax.dynamic_slice_in_dim(amps, cd_tile, 1, 1)[:, 0, :]
                    term = jnp.dot(tile_amps, ints_dev[row_index, col_index, slot], preferred_element_type=jnp.float32)
                    place = ab_dev[row_index, col_index, slot].astype(jnp.int32)
                    old = lax.dynamic_slice_in_dim(inner, place, 1, 1)
                    return lax.dynamic_update_slice_in_dim(inner, old + term[:, None, :], place, 1)

                return lax.cond(slot < count_dev[row_index, col_index], add_term, lambda inner: inner, acc)

            total = lax.fori_loop(0, DEVICE_SLOTS, one_slot, total)
            return total, None

        start = jnp.zeros((occ, PAIR_TILES_ROW, TILE_PAIRS), jnp.float32)
        total, _ = lax.scan(one_col, start, jnp.arange(N_COL, dtype=jnp.int32))
        return total

    blocks = lax.map(one_row, jnp.arange(N_ROW, dtype=jnp.int32))
    whole = jnp.transpose(blocks, (1, 0, 2, 3)).reshape(occ, N_ROW * PAIR_TILES_ROW, TILE_PAIRS)
    return whole.astype(jnp.bfloat16)
```

```python
import functools

import jax
import jax.numpy as jnp
from jax import lax
from jax.experimental import pallas as pl
from jax.experimental.pallas import tpu as pltpu
from jax.sharding import PartitionSpec as P

CD_COL = 8
PAIR_TILES_ROW = 8
CHUNKS = 2
LANES = 128
LEVELS = 32000.0
STEPS = 64.0
SMALLEST = 2.0**-110
VMEM_LIMIT = 48 * 1024 * 1024

F32 = jnp.float32
BF16 = jnp.bfloat16
I16 = jnp.int16

IN_VMEM = pl.BlockSpec(memory_space=pltpu.VMEM)
IN_SMEM = pl.BlockSpec(memory_space=pltpu.SMEM)
IN_HBM = pl.BlockSpec(memory_space=pl.ANY)


def held(x):
    return pltpu.with_memory_space_constraint(x, pltpu.VMEM)


def kernel_call(body, outs, ins, scratch=(), flops=0, moved=0, name=None):
    return pl.pallas_call(
        body,
        out_shape=outs,
        in_specs=ins,
        out_specs=jax.tree.map(lambda _: IN_VMEM, outs),
        scratch_shapes=list(scratch),
        compiler_params=pltpu.CompilerParams(vmem_limit_bytes=VMEM_LIMIT),
        cost_estimate=pl.CostEstimate(flops=flops, bytes_accessed=moved, transcendentals=0),
        name=name,
    )


def code(block):
    top = jnp.maximum(jnp.max(jnp.abs(block), axis=0, keepdims=True), SMALLEST)
    exponent = jnp.ceil(jnp.log2(top) * STEPS)
    scaled = block * (LEVELS * jnp.exp2(exponent * (-1.0 / STEPS)))
    return jnp.round(scaled).astype(jnp.int32).astype(I16), exponent


def store_exponents(ref, at, rows):
    tiles = len(rows)
    block = jnp.concatenate(list(rows) + [jnp.zeros_like(rows[0])] * (16 - tiles), axis=0)
    ref[at] = block.astype(jnp.int32).astype(I16)


def scales(exponents):
    return jnp.exp2(exponents.astype(jnp.int32).astype(F32) * (1.0 / STEPS)) * (1.0 / LEVELS)


def decode(block, scale):
    return block.astype(jnp.int32).astype(F32) * scale


def split_kernel(parts, here_ref, amps_ref, *refs):
    outs, flat = refs[:-1], refs[-1]
    rows, tiles, width = amps_ref.shape
    chunks, each = len(outs), outs[0].shape[2]
    lanes = flat.shape[2]
    for half in range(width // lanes):
        columns = pl.ds(half * lanes, lanes)
        flat[half] = amps_ref[:, :, columns].astype(F32).reshape(rows * tiles, lanes)
    for step in range(parts):
        part = lax.rem(here_ref[0] + step, parts)
        for chunk in range(chunks):
            for tile in range(tiles):
                first = (part * (rows // parts) + chunk * each) * tiles + tile
                for half in range(width // lanes):
                    picked = flat[half, pl.ds(first, each, stride=tiles), :]
                    outs[chunk][step, tile, :, pl.ds(half * lanes, lanes)] = picked.astype(BF16)


def table_kernel(cd_ref, ab_ref, count_ref, ints_ref, table_ref, present, sems):
    slots = cd_ref.shape[0]
    pairs = present.shape[0]
    count = count_ref[0]

    def copy(slot):
        place = ab_ref[slot] * CD_COL + cd_ref[slot]
        return pltpu.make_async_copy(ints_ref.at[slot], table_ref.at[place], sems.at[slot])

    def clear(pair, carry):
        present[pair] = 0
        return carry

    def start(slot, carry):
        copy(slot).start()
        present[ab_ref[slot] * CD_COL + cd_ref[slot]] = 1
        return carry

    def fill(pair, carry):
        @pl.when(present[pair] == 0)
        def _():
            table_ref[pair] = jnp.zeros(table_ref.shape[1:], table_ref.dtype)

        return carry

    def finish(slot, carry):
        copy(slot).wait()
        return carry

    lax.fori_loop(0, pairs, clear, 0)
    lax.fori_loop(0, count, start, 0)
    lax.fori_loop(0, pairs, fill, 0)
    lax.fori_loop(0, count, finish, 0)


def product_kernel(blocks, *refs):
    amps_refs, table_ref = refs[:blocks], refs[blocks]
    parts, tiles, each, width = amps_refs[0].shape
    keep_ref = refs[blocks + 1]
    send_refs = refs[blocks + 2 : blocks + 1 + parts]
    left = refs[-1]
    ab_tiles = table_ref.shape[0] // tiles
    for tile in range(tiles):
        for block in range(blocks):
            for part in range(parts):
                at = (block * parts + part) * each
                left[at : at + each, tile * width : (tile + 1) * width] = amps_refs[block][part, tile]
    exponents = {}
    for ab in range(ab_tiles):
        right = table_ref[ab * tiles : (ab + 1) * tiles].reshape(tiles * width, table_ref.shape[2])
        total = jnp.dot(left[...], right, preferred_element_type=F32)
        for block in range(blocks):
            for part in range(parts):
                at = (block * parts + part) * each
                piece = total[at : at + each]
                if part == 0:
                    keep_ref[block, ab] = piece
                else:
                    coded, exponent = code(piece)
                    send_refs[part - 1][block, ab * each : (ab + 1) * each] = coded
                    exponents.setdefault((block, part), []).append(exponent)
    for (block, part), rows in exponents.items():
        store_exponents(send_refs[part - 1].at[block], pl.ds(ab_tiles * each, 16), rows)


def pair_kernel(places_ref, keep_ref, *refs):
    blocks, ab_tiles, each, width = keep_ref.shape
    received = refs[: len(refs) - blocks]
    own_ref, send_refs = refs[len(received)], refs[len(received) + 1 :]
    for step in range(blocks):
        block = places_ref[step]
        factors = [scales(ref[block, pl.ds(ab_tiles * each, 16)]) for ref in received]
        exponents = []
        for ab in range(ab_tiles):
            total = keep_ref[block, ab]
            for ref, factor in zip(received, factors):
                total = total + decode(ref[block, ab * each : (ab + 1) * each], factor[ab : ab + 1])
            if step == 0:
                own_ref[ab] = total
            else:
                coded, exponent = code(total)
                send_refs[step - 1][ab * each : (ab + 1) * each] = coded
                exponents.append(exponent)
        if step:
            store_exponents(send_refs[step - 1], pl.ds(ab_tiles * each, 16), exponents)


def last_kernel(chunks, *refs):
    flat, out_ref = refs[-1], refs[-2]
    per = (len(refs) - 2) // chunks
    rows, ab_tiles, width = out_ref.shape
    lanes = flat.shape[2]
    for chunk in range(chunks):
        own_ref, received = refs[chunk * per], refs[chunk * per + 1 : (chunk + 1) * per]
        each = own_ref.shape[1]
        factors = [scales(ref[pl.ds(ab_tiles * each, 16)]) for ref in received]
        for ab in range(ab_tiles):
            total = own_ref[ab]
            for ref, factor in zip(received, factors):
                total = total + decode(ref[ab * each : (ab + 1) * each], factor[ab : ab + 1])
            for half in range(width // lanes):
                piece = total[:, half * lanes : (half + 1) * lanes]
                flat[half, pl.ds(chunk * each * ab_tiles + ab, each, stride=ab_tiles), :] = piece
    for half in range(width // lanes):
        whole = flat[half].reshape(rows, ab_tiles, lanes)
        out_ref[:, :, pl.ds(half * lanes, lanes)] = whole.astype(out_ref.dtype)


def shards(n_row, n_col, amps, ints, task_cd, task_ab, task_count):
    n_x = n_col // n_row
    n_z = n_row
    n_y = n_row // 2
    rows, tiles, width = amps.shape
    out_rows = rows // n_x
    each = out_rows // CHUNKS
    row, col = lax.axis_index("row"), lax.axis_index("col")
    x, z = lax.rem(col, n_x), lax.div(col, n_x)

    def along_row(array, pairs):
        return lax.ppermute(array, "row", pairs)

    def along_x(array, step):
        pairs = [(c, c - c % n_x + (c % n_x + step) % n_x) for c in range(n_col)]
        return lax.ppermute(array, "col", pairs)

    def along_z(array, step):
        return lax.ppermute(array, "col", [(c, (c + step * n_x) % n_col) for c in range(n_col)])

    swap = [(r, r ^ 1) for r in range(n_row)]

    mine = kernel_call(
        functools.partial(split_kernel, n_x),
        [jax.ShapeDtypeStruct((n_x, tiles, each, width), BF16)] * CHUNKS,
        [IN_SMEM, IN_VMEM],
        [pltpu.VMEM((width // LANES, rows * tiles, LANES), F32)],
        name="split",
    )(x[None], amps)
    others = [
        [along_row(mine[q], [(r, (r + 2 * k) % n_row) for r in range(n_row)]) for k in range(1, n_y)]
        for q in range(CHUNKS)
    ]
    beside = [along_row(mine[q], swap) for q in range(CHUNKS)]
    pairs = PAIR_TILES_ROW * CD_COL
    table = pl.pallas_call(
        table_kernel,
        out_shape=pltpu.VMEM((pairs, width, ints.shape[2]), BF16),
        in_specs=[IN_SMEM, IN_SMEM, IN_SMEM, IN_HBM],
        out_specs=IN_VMEM,
        scratch_shapes=[pltpu.SMEM((pairs,), jnp.int32), pltpu.SemaphoreType.DMA((ints.shape[0],))],
        compiler_params=pltpu.CompilerParams(vmem_limit_bytes=VMEM_LIMIT),
        cost_estimate=pl.CostEstimate(flops=0, bytes_accessed=ints.size * 2, transcendentals=0),
        name="table",
    )(task_cd, task_ab, task_count, ints)

    places = []
    for step in range(n_z):
        wanted = lax.rem(z + step, n_z)
        far = lax.rem(row // 2 - wanted // 2 + n_y, n_y)
        places.append(2 * far + lax.rem(row + wanted, 2))
    places = jnp.stack(places).astype(jnp.int32)

    coded_rows = PAIR_TILES_ROW * each + 16
    last = []
    for q in range(CHUNKS):
        blocks = [mine[q], beside[q]]
        for other in others[q]:
            blocks += [other, along_row(other, swap)]
        keep, *sends = kernel_call(
            functools.partial(product_kernel, n_row),
            [jax.ShapeDtypeStruct((n_row, PAIR_TILES_ROW, each, width), F32)]
            + [jax.ShapeDtypeStruct((n_row, coded_rows, width), I16)] * (n_x - 1),
            [IN_VMEM] * (n_row + 1),
            [pltpu.VMEM((n_row * n_x * each, tiles * width), BF16)],
            flops=2 * n_row * n_x * each * tiles * width * PAIR_TILES_ROW * width,
            moved=0,
            name="product",
        )(*blocks, held(table))
        received = [along_x(send, step) for step, send in zip(range(1, n_x), sends)]
        own, *sends = kernel_call(
            pair_kernel,
            [jax.ShapeDtypeStruct((PAIR_TILES_ROW, each, width), F32)]
            + [jax.ShapeDtypeStruct((coded_rows, width), I16)] * (n_z - 1),
            [IN_SMEM] + [IN_VMEM] * n_x,
            name="pairs",
        )(places, keep, *received)
        last += [own] + [along_z(send, step) for step, send in zip(range(1, n_z), sends)]
    return kernel_call(
        functools.partial(last_kernel, CHUNKS),
        jax.ShapeDtypeStruct((out_rows, PAIR_TILES_ROW, width), BF16),
        [IN_VMEM] * len(last),
        [pltpu.VMEM((width // LANES, out_rows * PAIR_TILES_ROW, LANES), F32)],
        name="last",
    )(*last)


def solution(mesh):
    return jax.shard_map(
        functools.partial(shards, mesh.shape["row"], mesh.shape["col"]),
        mesh=mesh,
        in_specs=(
            P("row", "col", None),
            P(("row", "col"), None, None),
            P(("row", "col")),
            P(("row", "col")),
            P(("row", "col")),
        ),
        out_specs=P("col", "row", None),
        check_vma=False,
    )
```

```python
import functools

import jax
import jax.numpy as jnp
from jax import lax
from jax.experimental import pallas as pl
from jax.experimental.pallas import tpu as pltpu
from jax.sharding import PartitionSpec as P

CD_COL = 8
PAIR_TILES_ROW = 8
CHUNKS = 2
LOADS = 8
LANES = 128
LEVELS = 32000.0
STEPS = 64.0
SMALLEST = 2.0**-110
VMEM_LIMIT = 16 * 1024 * 1024

F32 = jnp.float32
BF16 = jnp.bfloat16
I16 = jnp.int16

IN_VMEM = pl.BlockSpec(memory_space=pltpu.VMEM)
IN_SMEM = pl.BlockSpec(memory_space=pltpu.SMEM)
IN_HBM = pl.BlockSpec(memory_space=pl.ANY)


def held(x):
    return pltpu.with_memory_space_constraint(x, pltpu.VMEM)


def after(x, *others):
    return lax.optimization_barrier((x, *others))[0]


def kernel_call(body, outs, ins, scratch=(), flops=0, moved=0, name=None, outputs=IN_VMEM):
    return pl.pallas_call(
        body,
        out_shape=outs,
        in_specs=ins,
        out_specs=outputs if outputs is not IN_VMEM else jax.tree.map(lambda _: IN_VMEM, outs),
        scratch_shapes=list(scratch),
        compiler_params=pltpu.CompilerParams(vmem_limit_bytes=VMEM_LIMIT),
        cost_estimate=pl.CostEstimate(flops=flops, bytes_accessed=moved, transcendentals=0),
        name=name,
    )


def code(block):
    top = jnp.maximum(jnp.max(jnp.abs(block), axis=0, keepdims=True), SMALLEST)
    exponent = jnp.ceil(jnp.log2(top) * STEPS)
    scaled = block * (LEVELS * jnp.exp2(exponent * (-1.0 / STEPS)))
    return jnp.round(scaled).astype(jnp.int32).astype(I16), exponent


def store_exponents(ref, at, rows):
    tiles = len(rows)
    block = jnp.concatenate(list(rows) + [jnp.zeros_like(rows[0])] * (16 - tiles), axis=0)
    ref[at] = block.astype(jnp.int32).astype(I16)


def scales(exponents):
    return jnp.exp2(exponents.astype(jnp.int32).astype(F32) * (1.0 / STEPS)) * (1.0 / LEVELS)


def decode(block, scale):
    return block.astype(jnp.int32).astype(F32) * scale


def split_kernel(parts, here_ref, amps_ref, *refs):
    outs, flat = refs[:-1], refs[-1]
    rows, tiles, width = amps_ref.shape
    lanes, each = flat.shape[2], rows // parts
    for half in range(width // lanes):
        columns = pl.ds(half * lanes, lanes)
        flat[half] = amps_ref[:, :, columns].astype(F32).reshape(rows * tiles, lanes)
    for step in range(parts):
        part = lax.rem(here_ref[0] + step, parts)
        for tile in range(tiles):
            first = part * each * tiles + tile
            for half in range(width // lanes):
                picked = flat[half, pl.ds(first, each, stride=tiles), :]
                outs[step][tile, :, pl.ds(half * lanes, lanes)] = picked.astype(BF16)


def load_kernel(pieces, cd_ref, ab_ref, count_ref, ints_ref, slots_ref, table_ref, sems):
    per = ints_ref.shape[0] // pieces
    pairs = slots_ref.shape[0] // 2
    count = count_ref[0]
    live = lax.div(count + per - 1, per)

    def copy(piece):
        part = pl.ds(piece * per, per)
        return pltpu.make_async_copy(ints_ref.at[part], table_ref.at[part], sems.at[piece])

    def start(piece, carry):
        copy(piece).start()
        return carry

    def clear(pair, carry):
        slots_ref[pair] = 0
        slots_ref[pairs + pair] = CD_COL
        return carry

    def note(slot, carry):
        pair = ab_ref[slot] * CD_COL + cd_ref[slot]
        slots_ref[pair] = slot
        slots_ref[pairs + pair] = cd_ref[slot]
        return carry

    def finish(piece, carry):
        copy(piece).wait()
        return carry

    lax.fori_loop(0, live, start, 0)
    lax.fori_loop(0, pairs, clear, 0)
    lax.fori_loop(0, count, note, 0)
    lax.fori_loop(0, live, finish, 0)


def multiply(amps_refs, slots_ref, table_ref, left, use):
    tiles, each, width = amps_refs[0].shape
    pairs = slots_ref.shape[0] // 2
    rows = each * len(amps_refs)
    for tile in range(tiles):
        for block, ref in enumerate(amps_refs):
            left[tile, block * each : (block + 1) * each] = ref[tile]
    left[tiles] = jnp.zeros((rows, width), BF16)
    for ab in range(pairs // tiles):
        total = jnp.zeros((rows, table_ref.shape[2]), F32)
        for tile in range(tiles):
            pair = ab * tiles + tile
            total = total + jnp.dot(
                left[slots_ref[pairs + pair]], table_ref[slots_ref[pair]], preferred_element_type=F32
            )
        use(ab, total)


def keep_kernel(blocks, *refs):
    slots_ref, table_ref, keep_ref, left = refs[blocks:]
    each = refs[0].shape[1]

    def use(ab, total):
        for block in range(blocks):
            keep_ref[block, ab] = total[block * each : (block + 1) * each]

    multiply(refs[:blocks], slots_ref, table_ref, left, use)


def send_kernel(blocks, chunks, *refs):
    slots_ref, table_ref = refs[blocks : blocks + 2]
    send_refs, left = refs[blocks + 2 : -1], refs[-1]
    each = refs[0].shape[1] // chunks
    exponents = {}
    tiles = slots_ref.shape[0] // 2 // CD_COL

    def use(ab, total):
        for block in range(blocks):
            for chunk in range(chunks):
                at = (block * chunks + chunk) * each
                coded, exponent = code(total[at : at + each])
                send_refs[chunk][block, ab * each : (ab + 1) * each] = coded
                exponents.setdefault((block, chunk), []).append(exponent)

    multiply(refs[:blocks], slots_ref, table_ref, left, use)
    for (block, chunk), rows in exponents.items():
        store_exponents(send_refs[chunk].at[block], pl.ds(tiles * each, 16), rows)


def pair_kernel(chunk, near, places_ref, keep_ref, *refs):
    blocks, ab_tiles, _, width = keep_ref.shape
    sums = refs[-1]
    each = sums.shape[2]
    received = refs[: len(refs) - 1 - blocks]
    own_ref, send_refs = refs[len(received)], refs[len(received) + 1 : -1]
    half = len(received) // 2
    for block in range(blocks):
        mine = received[:half] if block < near else received[half:]
        at = block if block < near else block - near
        factors = [scales(ref[at, pl.ds(ab_tiles * each, 16)]) for ref in mine]
        for ab in range(ab_tiles):
            total = keep_ref[block, ab, chunk * each : (chunk + 1) * each]
            for ref, factor in zip(mine, factors):
                total = total + decode(ref[at, ab * each : (ab + 1) * each], factor[ab : ab + 1])
            sums[block, ab] = total
    own_ref[...] = sums[places_ref[0]]
    for step in range(1, blocks):
        exponents = []
        for ab in range(ab_tiles):
            coded, exponent = code(sums[places_ref[step], ab])
            send_refs[step - 1][ab * each : (ab + 1) * each] = coded
            exponents.append(exponent)
        store_exponents(send_refs[step - 1], pl.ds(ab_tiles * each, 16), exponents)


def last_kernel(chunks, *refs):
    flat, out_ref = refs[-1], refs[-2]
    per = (len(refs) - 2) // chunks
    rows, ab_tiles, width = out_ref.shape
    lanes = flat.shape[2]
    for chunk in range(chunks):
        own_ref, received = refs[chunk * per], refs[chunk * per + 1 : (chunk + 1) * per]
        each = own_ref.shape[1]
        factors = [scales(ref[pl.ds(ab_tiles * each, 16)]) for ref in received]
        for ab in range(ab_tiles):
            total = own_ref[ab]
            for ref, factor in zip(received, factors):
                total = total + decode(ref[ab * each : (ab + 1) * each], factor[ab : ab + 1])
            for half in range(width // lanes):
                piece = total[:, half * lanes : (half + 1) * lanes]
                flat[half, pl.ds(chunk * each * ab_tiles + ab, each, stride=ab_tiles), :] = piece
    for half in range(width // lanes):
        whole = flat[half].reshape(rows, ab_tiles, lanes)
        out_ref[:, :, pl.ds(half * lanes, lanes)] = whole.astype(out_ref.dtype)


def shards(n_row, n_col, amps, ints, task_cd, task_ab, task_count):
    n_x = n_col // n_row
    n_z = n_row
    n_y = n_row // 2
    rows, tiles, width = amps.shape
    out_rows = rows // n_x
    each = out_rows // CHUNKS
    pairs = PAIR_TILES_ROW * CD_COL
    coded_rows = PAIR_TILES_ROW * each + 16
    row, col = lax.axis_index("row"), lax.axis_index("col")
    x, z = lax.rem(col, n_x), lax.div(col, n_x)
    other_parts = range(1, n_x)

    def along_y(array, step):
        return lax.ppermute(array, "row", [(r, (r + 2 * step) % n_row) for r in range(n_row)])

    def to_partner(array):
        return lax.ppermute(array, "row", [(r, r ^ 1) for r in range(n_row)])

    def along_x(array, step):
        pairs = [(c, c - c % n_x + (c % n_x + step) % n_x) for c in range(n_col)]
        return lax.ppermute(array, "col", pairs)

    def along_z(array, step):
        return lax.ppermute(array, "col", [(c, (c + step * n_x) % n_col) for c in range(n_col)])

    def send_products(blocks):
        return kernel_call(
            functools.partial(send_kernel, len(blocks), CHUNKS),
            [pltpu.VMEM((len(blocks), coded_rows, width), I16)] * CHUNKS,
            [IN_VMEM] * len(blocks) + [IN_SMEM, IN_VMEM],
            [pltpu.VMEM((tiles + 1, len(blocks) * out_rows, width), BF16)],
            flops=2 * len(blocks) * out_rows * tiles * width * PAIR_TILES_ROW * width,
            name="send_products",
        )(*map(held, blocks), slots, held(table))

    places = []
    for step in range(n_z):
        wanted = lax.rem(z + step, n_z)
        far = lax.rem(row // 2 - wanted // 2 + n_y, n_y)
        places.append(2 * far + lax.rem(row + wanted, 2))
    places = jnp.stack(places).astype(jnp.int32)

    mine = kernel_call(
        functools.partial(split_kernel, n_x),
        [pltpu.VMEM((tiles, out_rows, width), BF16)] * n_x,
        [IN_SMEM, IN_VMEM],
        [pltpu.VMEM((width // LANES, rows * tiles, LANES), F32)],
        name="split",
    )(x[None], amps)
    order = [*other_parts, 0]
    beside = {part: to_partner(mine[part]) for part in order}
    far = {part: [along_y(mine[part], k) for k in range(1, n_y)] for part in order}
    slots, table = kernel_call(
        functools.partial(load_kernel, LOADS),
        [pltpu.SMEM((2 * pairs,), jnp.int32), pltpu.VMEM(ints.shape, BF16)],
        [IN_SMEM, IN_SMEM, IN_SMEM, IN_HBM],
        [pltpu.SemaphoreType.DMA((LOADS,))],
        moved=ints.size * 2,
        outputs=[IN_SMEM, IN_VMEM],
        name="load",
    )(task_cd, task_ab, task_count, pltpu.with_memory_space_constraint(ints, pltpu.HBM))

    near_sends = [send_products([mine[part], beside[part]]) for part in other_parts]
    x_sent = {}
    near_received = [[along_x(sends[0], part) for part, sends in zip(other_parts, near_sends)]]

    def fetch(part, *ties):
        blocks = []
        for array in far[part]:
            array = after(array, *ties)
            blocks += [array, to_partner(array)]
        return blocks

    far_blocks = {part: fetch(part, near_sends[-1][0]) for part in other_parts}
    far_sends = [send_products(far_blocks[part]) for part in other_parts]
    far_received = [[along_x(sends[0], part) for part, sends in zip(other_parts, far_sends)]]
    for q in range(1, CHUNKS):
        near_received.append(
            [along_x(after(sends[q], far_sends[-1][0]), part) for part, sends in zip(other_parts, near_sends)]
        )
        far_received.append([along_x(sends[q], part) for part, sends in zip(other_parts, far_sends)])
    far_blocks[0] = fetch(0, far_sends[-1][0])
    blocks = [mine[0], beside[0], *far_blocks[0]]
    keep = kernel_call(
        functools.partial(keep_kernel, n_row),
        pltpu.VMEM((n_row, PAIR_TILES_ROW, out_rows, width), F32),
        [IN_VMEM] * n_row + [IN_SMEM, IN_VMEM],
        [pltpu.VMEM((tiles + 1, n_row * out_rows, width), BF16)],
        flops=2 * n_row * out_rows * tiles * width * PAIR_TILES_ROW * width,
        name="keep_products",
    )(*map(held, blocks), slots, held(table))

    last = []
    for q in range(CHUNKS):
        own, *sends = kernel_call(
            functools.partial(pair_kernel, q, 2),
            [pltpu.VMEM((PAIR_TILES_ROW, each, width), F32)] + [pltpu.VMEM((coded_rows, width), I16)] * (n_z - 1),
            [IN_SMEM] + [IN_VMEM] * (2 * n_x - 1),
            [pltpu.VMEM((n_row, PAIR_TILES_ROW, each, width), F32)],
            name="pairs",
        )(places, held(keep), *map(held, near_received[q]), *map(held, far_received[q]))
        last += [own] + [along_z(send, step) for step, send in zip(range(1, n_z), sends)]
    return kernel_call(
        functools.partial(last_kernel, CHUNKS),
        jax.ShapeDtypeStruct((out_rows, PAIR_TILES_ROW, width), BF16),
        [IN_VMEM] * len(last),
        [pltpu.VMEM((width // LANES, out_rows * PAIR_TILES_ROW, LANES), F32)],
        name="last",
    )(*map(held, last))


def solution(mesh):
    return jax.shard_map(
        functools.partial(shards, mesh.shape["row"], mesh.shape["col"]),
        mesh=mesh,
        in_specs=(
            P("row", "col", None),
            P(("row", "col"), None, None),
            P(("row", "col")),
            P(("row", "col")),
            P(("row", "col")),
        ),
        out_specs=P("col", "row", None),
        check_vma=False,
    )
```

```python
import functools

import jax
import jax.numpy as jnp
from jax import lax
from jax.experimental import pallas as pl
from jax.experimental.pallas import tpu as pltpu
from jax.sharding import PartitionSpec as P

CD_COL = 8
PAIR_TILES_ROW = 8
PARTS = (2, 1, 1)
LOADS = 8
LANES = 128
LEVELS = 32000.0
STEPS = 64.0
SMALLEST = 2.0**-110
VMEM_LIMIT = 16 * 1024 * 1024

F32 = jnp.float32
BF16 = jnp.bfloat16
I16 = jnp.int16

IN_VMEM = pl.BlockSpec(memory_space=pltpu.VMEM)
IN_SMEM = pl.BlockSpec(memory_space=pltpu.SMEM)
IN_HBM = pl.BlockSpec(memory_space=pl.ANY)


def held(x):
    return pltpu.with_memory_space_constraint(x, pltpu.VMEM)


def after(x, *others):
    return lax.optimization_barrier((x, *others))[0]


def kernel_call(body, outs, ins, scratch=(), name=None, outputs=IN_VMEM):
    return pl.pallas_call(
        body,
        out_shape=outs,
        in_specs=ins,
        out_specs=outputs if outputs is not IN_VMEM else jax.tree.map(lambda _: IN_VMEM, outs),
        scratch_shapes=list(scratch),
        compiler_params=pltpu.CompilerParams(vmem_limit_bytes=VMEM_LIMIT),
        cost_estimate=pl.CostEstimate(flops=1, bytes_accessed=1, transcendentals=0),
        name=name,
    )


def code(block):
    top = jnp.maximum(jnp.max(jnp.abs(block), axis=0, keepdims=True), SMALLEST)
    exponent = jnp.ceil(jnp.log2(top) * STEPS)
    scaled = block * (LEVELS * jnp.exp2(exponent * (-1.0 / STEPS)))
    return jnp.round(scaled).astype(jnp.int32).astype(I16), exponent


def store_exponents(ref, at, rows):
    tiles = len(rows)
    block = jnp.concatenate(list(rows) + [jnp.zeros_like(rows[0])] * (16 - tiles), axis=0)
    ref[at] = block.astype(jnp.int32).astype(I16)


def scales(exponents):
    return jnp.exp2(exponents.astype(jnp.int32).astype(F32) * (1.0 / STEPS)) * (1.0 / LEVELS)


def decode(block, scale):
    return block.astype(jnp.int32).astype(F32) * scale


def begin_kernel(parts, pieces, count_ref, cd_hbm, ab_hbm, amps_hbm, ints_hbm, *refs):
    outs, (slots_ref, table_ref, amps, flat, cd, ab, sems) = refs[:parts], refs[parts:]
    rows, tiles, width = amps.shape
    lanes, each = flat.shape[2], rows // parts
    per = ints_hbm.shape[0] // pieces
    pairs = slots_ref.shape[0] // 2
    copies = [pltpu.make_async_copy(amps_hbm, amps, sems.at[0])]
    copies += [pltpu.make_async_copy(cd_hbm, cd, sems.at[1]), pltpu.make_async_copy(ab_hbm, ab, sems.at[2])]
    for piece in range(pieces):
        part = pl.ds(piece * per, per)
        copies.append(pltpu.make_async_copy(ints_hbm.at[part], table_ref.at[part], sems.at[3 + piece]))
    for copy in copies:
        copy.start()

    def clear(pair, carry):
        slots_ref[pair] = 0
        slots_ref[pairs + pair] = CD_COL
        return carry

    def note(slot, carry):
        pair = ab[slot] * CD_COL + cd[slot]
        slots_ref[pair] = slot
        slots_ref[pairs + pair] = cd[slot]
        return carry

    lax.fori_loop(0, pairs, clear, 0)
    copies[0].wait()
    for half in range(width // lanes):
        columns = pl.ds(half * lanes, lanes)
        flat[half] = amps[:, :, columns].astype(F32).reshape(rows * tiles, lanes)
    here = lax.rem(lax.axis_index("col"), parts)
    for step in range(parts):
        part = lax.rem(here + step, parts)
        for tile in range(tiles):
            first = part * each * tiles + tile
            for half in range(width // lanes):
                picked = flat[half, pl.ds(first, each, stride=tiles), :]
                outs[step][tile, :, pl.ds(half * lanes, lanes)] = picked.astype(BF16)
    copies[1].wait()
    copies[2].wait()
    lax.fori_loop(0, count_ref[0], note, 0)
    for copy in copies[3:]:
        copy.wait()


def multiply(amps_refs, slots_ref, table_ref, left, use):
    tiles, each, width = amps_refs[0].shape
    pairs = slots_ref.shape[0] // 2
    rows = each * len(amps_refs)
    for tile in range(tiles):
        for block, ref in enumerate(amps_refs):
            left[tile, block * each : (block + 1) * each] = ref[tile]
    left[tiles] = jnp.zeros((rows, width), BF16)
    for ab in range(pairs // tiles):
        total = jnp.zeros((rows, table_ref.shape[2]), F32)
        for tile in range(tiles):
            pair = ab * tiles + tile
            total = total + jnp.dot(
                left[slots_ref[pairs + pair]], table_ref[slots_ref[pair]], preferred_element_type=F32
            )
        use(ab, total)


def keep_kernel(blocks, *refs):
    slots_ref, table_ref, keep_ref, left = refs[blocks:]
    each = refs[0].shape[1]

    def use(ab, total):
        for block in range(blocks):
            keep_ref[block, ab] = total[block * each : (block + 1) * each]

    multiply(refs[:blocks], slots_ref, table_ref, left, use)


def send_kernel(blocks, sizes, stacked, *refs):
    slots_ref, table_ref = refs[blocks : blocks + 2]
    send_refs, left = refs[blocks + 2 : -1], refs[-1]
    out_rows = refs[0].shape[1]
    exponents = {}
    tiles = slots_ref.shape[0] // 2 // CD_COL
    starts = [sum(sizes[:chunk]) for chunk in range(len(sizes))]

    def place(block, chunk):
        if stacked and chunk:
            return send_refs[1].at[chunk - 1, block]
        return send_refs[chunk].at[block]

    def use(ab, total):
        for block in range(blocks):
            for chunk, each in enumerate(sizes):
                at = block * out_rows + starts[chunk]
                coded, exponent = code(total[at : at + each])
                place(block, chunk)[ab * each : (ab + 1) * each] = coded
                exponents.setdefault((block, chunk), []).append(exponent)

    multiply(refs[:blocks], slots_ref, table_ref, left, use)
    for (block, chunk), rows in exponents.items():
        store_exponents(place(block, chunk), pl.ds(tiles * sizes[chunk], 16), rows)


def add_decoded(total, ref, ab, ab_tiles, factor):
    each = total.shape[0]
    return total + decode(ref[ab * each : (ab + 1) * each], factor[ab : ab + 1])


def tail_scales(ref, ab_tiles, each):
    return scales(ref[pl.ds(ab_tiles * each, 16)])


def code_into(ref, tiles):
    each = tiles[0].shape[0]
    exponents = []
    for ab, tile in enumerate(tiles):
        coded, exponent = code(tile)
        ref[ab * each : (ab + 1) * each] = coded
        exponents.append(exponent)
    store_exponents(ref, pl.ds(len(tiles) * each, 16), exponents)


def pair_kernel(start, stack, near_ref, far_ref, *refs):
    near, ab_tiles = near_ref.shape[:2]
    blocks = near + far_ref.shape[0]
    received, (kept_ref, sent_ref, sums) = refs[:-3], refs[-3:]
    each = sums.shape[2]
    half = len(received) // 2
    near_received = [ref if stack is None else ref.at[stack] for ref in received[:half]]
    row, col = lax.axis_index("row"), lax.axis_index("col")
    n_y, z = blocks // 2, lax.div(col, half + 1)
    places = []
    for m in range(blocks):
        wanted = z ^ m
        away = lax.rem(lax.div(row, 2) - lax.div(wanted, 2) + n_y, n_y)
        places.append(2 * away + lax.rem(row + wanted, 2))
    for block in range(blocks):
        keep_ref, mine = (near_ref, near_received) if block < near else (far_ref, received[half:])
        at = block if block < near else block - near
        factors = [tail_scales(ref.at[at], ab_tiles, each) for ref in mine]
        for ab in range(ab_tiles):
            total = keep_ref[at, ab, start : start + each]
            for ref, factor in zip(mine, factors):
                total = add_decoded(total, ref.at[at], ab, ab_tiles, factor)
            sums[block, ab] = total
    for m in range(0, blocks, 2):
        kept_ref[m // 2] = sums[places[m]]
        code_into(sent_ref.at[m // 2], [sums[places[m + 1], ab] for ab in range(ab_tiles)])


def halve_kernel(kept_ref, received_ref, next_ref, sent_ref):
    count, ab_tiles, each, width = kept_ref.shape
    for item in range(count):
        factor = tail_scales(received_ref.at[item], ab_tiles, each)
        tiles = [
            add_decoded(kept_ref[item, ab], received_ref.at[item], ab, ab_tiles, factor) for ab in range(ab_tiles)
        ]
        if item % 2:
            code_into(sent_ref.at[item // 2], tiles)
        else:
            for ab in range(ab_tiles):
                next_ref[item // 2, ab] = tiles[ab]


def last_kernel(*refs):
    flat, out_ref = refs[-1], refs[-2]
    rows, ab_tiles, width = out_ref.shape
    lanes = flat.shape[2]
    start = 0
    for kept_ref, received_ref in zip(refs[:-2:2], refs[1:-2:2]):
        each = kept_ref.shape[2]
        factor = tail_scales(received_ref.at[0], ab_tiles, each)
        for ab in range(ab_tiles):
            total = add_decoded(kept_ref[0, ab], received_ref.at[0], ab, ab_tiles, factor)
            for half in range(width // lanes):
                piece = total[:, half * lanes : (half + 1) * lanes]
                flat[half, pl.ds(start * ab_tiles + ab, each, stride=ab_tiles), :] = piece
        start += each
    for half in range(width // lanes):
        whole = flat[half].reshape(rows, ab_tiles, lanes)
        out_ref[:, :, pl.ds(half * lanes, lanes)] = whole.astype(out_ref.dtype)


def chunk_sizes(rows):
    parts = PARTS
    while parts[-1] > 1 and (rows % sum(parts) or (rows // sum(parts)) % 16):
        parts = (1,) * (len(parts) - 1)
    if rows % sum(parts) or (rows // sum(parts)) % 16:
        parts = (1,)
    return [rows // sum(parts) * part for part in parts]


def shards(n_row, n_col, amps, ints, task_cd, task_ab, task_count):
    n_x = n_col // n_row
    n_z = n_row
    n_y = n_row // 2
    rows, tiles, width = amps.shape
    out_rows = rows // n_x
    sizes = chunk_sizes(out_rows)
    pairs = PAIR_TILES_ROW * CD_COL
    other_parts = range(1, n_x)

    def along_y(array, step):
        return lax.ppermute(array, "row", [(r, (r + 2 * step) % n_row) for r in range(n_row)])

    def to_partner(array):
        return lax.ppermute(array, "row", [(r, r ^ 1) for r in range(n_row)])

    def along_x(array, step):
        pairs = [(c, c - c % n_x + (c % n_x + step) % n_x) for c in range(n_col)]
        return lax.ppermute(array, "col", pairs)

    def along_z(array, bit):
        return lax.ppermute(array, "col", [(c, (c // n_x ^ bit) * n_x + c % n_x) for c in range(n_col)])

    def coded(each, *lead):
        return pltpu.VMEM((*lead, PAIR_TILES_ROW * each + 16, width), I16)

    def summed(each, *lead):
        return pltpu.VMEM((*lead, PAIR_TILES_ROW, each, width), F32)

    def send_products(blocks, stacked):
        count = len(blocks)
        outs = [coded(each, count) for each in sizes]
        if stacked:
            outs = outs[:1] + [coded(sizes[-1], len(sizes) - 1, count)]
        return kernel_call(
            functools.partial(send_kernel, count, sizes, stacked),
            outs,
            [IN_VMEM] * count + [IN_SMEM, IN_VMEM],
            [pltpu.VMEM((tiles + 1, count * out_rows, width), BF16)],
            name="send_products",
        )(*map(held, blocks), slots, held(table))

    def keep_products(blocks):
        return kernel_call(
            functools.partial(keep_kernel, len(blocks)),
            pltpu.VMEM((len(blocks), PAIR_TILES_ROW, out_rows, width), F32),
            [IN_VMEM] * len(blocks) + [IN_SMEM, IN_VMEM],
            [pltpu.VMEM((tiles + 1, len(blocks) * out_rows, width), BF16)],
            name="keep_products",
        )(*map(held, blocks), slots, held(table))

    *mine, slots, table = pl.pallas_call(
        functools.partial(begin_kernel, n_x, LOADS),
        out_shape=[pltpu.VMEM((tiles, out_rows, width), BF16)] * n_x
        + [pltpu.SMEM((2 * pairs,), jnp.int32), pltpu.VMEM(ints.shape, BF16)],
        in_specs=[IN_SMEM] + [IN_HBM] * 4,
        out_specs=[IN_VMEM] * n_x + [IN_SMEM, IN_VMEM],
        scratch_shapes=[
            pltpu.VMEM(amps.shape, BF16),
            pltpu.VMEM((width // LANES, rows * tiles, LANES), F32),
            pltpu.SMEM(task_cd.shape, jnp.int32),
            pltpu.SMEM(task_ab.shape, jnp.int32),
            pltpu.SemaphoreType.DMA((3 + LOADS,)),
        ],
        compiler_params=pltpu.CompilerParams(vmem_limit_bytes=VMEM_LIMIT),
        cost_estimate=pl.CostEstimate(flops=1, bytes_accessed=1, transcendentals=0),
        name="begin",
    )(task_count, *(pltpu.with_memory_space_constraint(v, pltpu.HBM) for v in (task_cd, task_ab, amps, ints)))
    order = [*other_parts, 0]
    beside = {part: to_partner(mine[part]) for part in order}
    far = {part: [along_y(mine[part], k) for k in range(1, n_y)] for part in order}
    stacked = len(sizes) > 2
    near_sends = [send_products([mine[part], beside[part]], stacked) for part in other_parts]
    near_received = [[along_x(group, part) for part, group in zip(other_parts, groups)] for groups in zip(*near_sends)]
    near_keep = keep_products([after(mine[0], near_sends[-1][0]), beside[0]])

    def fetch(part, *ties):
        blocks = []
        for array in far[part]:
            array = after(array, *ties)
            blocks += [array, to_partner(array)]
        return blocks

    far_blocks = {part: fetch(part, near_keep) for part in other_parts}
    far_blocks = {part: [after(v, near_received[0][-1]) for v in blocks] for part, blocks in far_blocks.items()}
    far_sends = [send_products(far_blocks[part], False) for part in other_parts]
    far_received = []
    for q in range(len(sizes)):
        ties = near_received[1] if q else []
        far_received.append([along_x(after(sends[q], *ties), part) for part, sends in zip(other_parts, far_sends)])
    far_keep = keep_products(fetch(0, far_sends[-1][0], near_received[-1][-1]))

    last = []
    for q, each in enumerate(sizes):
        group = min(q, len(near_received) - 1)
        kept, sent = kernel_call(
            functools.partial(pair_kernel, sum(sizes[:q]), q - 1 if stacked and q else None),
            [summed(each, n_z // 2), coded(each, n_z // 2)],
            [IN_VMEM] * (2 * n_x),
            [summed(each, n_z)],
            name="pairs",
        )(held(near_keep), held(far_keep), *map(held, near_received[group]), *map(held, far_received[q]))
        received = along_z(sent, 1)
        bit, count = 2, n_z // 2
        while count > 1:
            count //= 2
            kept, sent = kernel_call(
                halve_kernel, [summed(each, count), coded(each, count)], [IN_VMEM] * 2, name="halve"
            )(held(kept), held(received))
            received = along_z(sent, bit)
            bit *= 2
        last += [kept, received]
    return kernel_call(
        last_kernel,
        jax.ShapeDtypeStruct((out_rows, PAIR_TILES_ROW, width), BF16),
        [IN_VMEM] * len(last),
        [pltpu.VMEM((width // LANES, out_rows * PAIR_TILES_ROW, LANES), F32)],
        name="last",
    )(*map(held, last))


def solution(mesh):
    return jax.shard_map(
        functools.partial(shards, mesh.shape["row"], mesh.shape["col"]),
        mesh=mesh,
        in_specs=(
            P("row", "col", None),
            P(("row", "col"), None, None),
            P(("row", "col")),
            P(("row", "col")),
            P(("row", "col")),
        ),
        out_specs=P("col", "row", None),
        check_vma=False,
    )
```

```python
import functools

import jax
import jax.numpy as jnp
from jax import lax
from jax.experimental import pallas as pl
from jax.experimental.pallas import tpu as pltpu
from jax.sharding import PartitionSpec as P

CD_COL = 8
PAIR_TILES_ROW = 8
LOADS = 8
HINT = 3 * 10**9
LANES = 128
LEVELS = 32000.0
STEPS = 64.0
SMALLEST = 2.0**-110
VMEM_LIMIT = 16 * 1024 * 1024

F32 = jnp.float32
BF16 = jnp.bfloat16
I16 = jnp.int16

IN_VMEM = pl.BlockSpec(memory_space=pltpu.VMEM)
IN_SMEM = pl.BlockSpec(memory_space=pltpu.SMEM)
IN_HBM = pl.BlockSpec(memory_space=pl.ANY)


def held(x):
    return pltpu.with_memory_space_constraint(x, pltpu.VMEM)


def after(x, *others):
    return lax.optimization_barrier((x, *others))[0]


def kernel_call(body, outs, ins, scratch=(), name=None, hint=0, outputs=IN_VMEM):
    return pl.pallas_call(
        body,
        out_shape=outs,
        in_specs=ins,
        out_specs=outputs if outputs is not IN_VMEM else jax.tree.map(lambda _: IN_VMEM, outs),
        scratch_shapes=list(scratch),
        compiler_params=pltpu.CompilerParams(vmem_limit_bytes=VMEM_LIMIT),
        cost_estimate=pl.CostEstimate(flops=1 + hint, bytes_accessed=1, transcendentals=0),
        name=name,
    )


def code(block):
    top = jnp.maximum(jnp.max(jnp.abs(block), axis=0, keepdims=True), SMALLEST)
    exponent = jnp.ceil(jnp.log2(top) * STEPS)
    scaled = block * (LEVELS * jnp.exp2(exponent * (-1.0 / STEPS)))
    return jnp.round(scaled).astype(jnp.int32).astype(I16), exponent


def store_exponents(ref, at, rows):
    tiles = len(rows)
    block = jnp.concatenate(list(rows) + [jnp.zeros_like(rows[0])] * (16 - tiles), axis=0)
    ref[at] = block.astype(jnp.int32).astype(I16)


def scales(exponents):
    return jnp.exp2(exponents.astype(jnp.int32).astype(F32) * (1.0 / STEPS)) * (1.0 / LEVELS)


def decode(block, scale):
    return block.astype(jnp.int32).astype(F32) * scale


def split_kernel(parts, amps_hbm, *refs):
    outs, (amps, flat, sem) = refs[:-3], refs[-3:]
    rows, tiles, width = amps.shape
    lanes = flat.shape[2]
    copy = pltpu.make_async_copy(amps_hbm, amps, sem)
    copy.start()
    copy.wait()
    for half in range(width // lanes):
        columns = pl.ds(half * lanes, lanes)
        flat[half] = amps[:, :, columns].astype(F32).reshape(rows * tiles, lanes)
    here = lax.rem(lax.axis_index("col"), parts)
    start = 0
    for out in outs:
        each = out.shape[2]
        for step in range(parts):
            part = lax.rem(here + step, parts)
            for tile in range(tiles):
                first = (part * (rows // parts) + start) * tiles + tile
                for half in range(width // lanes):
                    picked = flat[half, pl.ds(first, each, stride=tiles), :]
                    out[step, tile, :, pl.ds(half * lanes, lanes)] = picked.astype(BF16)
        start += each


def load_kernel(pieces, count_ref, cd_hbm, ab_hbm, ints_hbm, slots_ref, table_ref, cd, ab, sems):
    per = ints_hbm.shape[0] // pieces
    pairs = slots_ref.shape[0] // 2
    copies = [pltpu.make_async_copy(cd_hbm, cd, sems.at[0]), pltpu.make_async_copy(ab_hbm, ab, sems.at[1])]
    for piece in range(pieces):
        part = pl.ds(piece * per, per)
        copies.append(pltpu.make_async_copy(ints_hbm.at[part], table_ref.at[part], sems.at[2 + piece]))
    for copy in copies:
        copy.start()

    def clear(pair, carry):
        slots_ref[pair] = 0
        slots_ref[pairs + pair] = CD_COL
        return carry

    def note(slot, carry):
        pair = ab[slot] * CD_COL + cd[slot]
        slots_ref[pair] = slot
        slots_ref[pairs + pair] = cd[slot]
        return carry

    lax.fori_loop(0, pairs, clear, 0)
    copies[0].wait()
    copies[1].wait()
    lax.fori_loop(0, count_ref[0], note, 0)
    for copy in copies[2:]:
        copy.wait()


def multiply(left, slots_ref, table_ref, use):
    tiles, rows = left.shape[0] - 1, left.shape[1]
    pairs = slots_ref.shape[0] // 2
    left[tiles] = jnp.zeros(left.shape[1:], BF16)
    for ab in range(pairs // tiles):
        total = jnp.zeros((rows, table_ref.shape[2]), F32)
        for tile in range(tiles):
            pair = ab * tiles + tile
            total = total + jnp.dot(
                left[slots_ref[pairs + pair]], table_ref[slots_ref[pair]], preferred_element_type=F32
            )
        use(ab, total)


def product_kernel(blocks, x_first, *refs):
    amps_refs, (slots_ref, table_ref) = refs[:blocks], refs[blocks : blocks + 2]
    keep_ref, send_refs, left = refs[blocks + 2], refs[blocks + 3 : -1], refs[-1]
    parts, tiles, each, _ = amps_refs[0].shape
    kept = keep_ref.shape[0]
    if x_first:
        order = [(block, part) for part in range(parts) for block in range(blocks)]
        for tile in range(tiles):
            for at, (block, part) in enumerate(order):
                left[tile, at * each : (at + 1) * each] = amps_refs[block][part, tile]
    else:
        swapped = lax.rem(lax.axis_index("row") + lax.div(lax.axis_index("col"), parts), 2) == 1
        for tile in range(tiles):
            for pair in range(blocks // 2):
                for part in range(parts):
                    even, odd = amps_refs[2 * pair][part, tile], amps_refs[2 * pair + 1][part, tile]
                    at = pair * parts + part
                    left[tile, at * each : (at + 1) * each] = jnp.where(swapped, odd, even)
                    at += kept
                    left[tile, at * each : (at + 1) * each] = jnp.where(swapped, even, odd)
    sends = [ref.at[item] for ref in send_refs for item in range(ref.shape[0])]
    exponents = [[] for _ in sends]

    def use(ab, total):
        for at in range(kept):
            keep_ref[at, ab] = total[at * each : (at + 1) * each]
        for at, ref in enumerate(sends):
            first = (kept + at) * each
            coded, exponent = code(total[first : first + each])
            ref[ab * each : (ab + 1) * each] = coded
            exponents[at].append(exponent)

    multiply(left, slots_ref, table_ref, use)
    for ref, rows in zip(sends, exponents):
        store_exponents(ref, pl.ds(len(rows) * each, 16), rows)


def add_decoded(total, ref, ab, ab_tiles, factor):
    each = total.shape[0]
    return total + decode(ref[ab * each : (ab + 1) * each], factor[ab : ab + 1])


def tail_scales(ref, ab_tiles, each):
    return scales(ref[pl.ds(ab_tiles * each, 16)])


def code_into(ref, tiles):
    each = tiles[0].shape[0]
    exponents = []
    for ab, tile in enumerate(tiles):
        coded, exponent = code(tile)
        ref[ab * each : (ab + 1) * each] = coded
        exponents.append(exponent)
    store_exponents(ref, pl.ds(len(tiles) * each, 16), exponents)


def x_pair_kernel(n_x, n_z, *refs):
    refs, (kept_ref, sent_ref, sums) = refs[:-3], refs[-3:]
    half = len(refs) // 2
    ab_tiles, each = sums.shape[1:3]
    at = 0
    for keep_ref, *received in (refs[:half], refs[half:]):
        for item in range(keep_ref.shape[0]):
            factors = [tail_scales(ref.at[item], ab_tiles, each) for ref in received]
            for ab in range(ab_tiles):
                total = keep_ref[item, ab]
                for ref, factor in zip(received, factors):
                    total = add_decoded(total, ref.at[item], ab, ab_tiles, factor)
                sums[at, ab] = total
            at += 1
    put_in_order(False, n_x, n_z, sums, kept_ref, sent_ref)


def put_in_order(z_first, n_x, n_z, sums, kept_ref, sent_ref):
    ab_tiles = sums.shape[1]
    row, z, n_y = lax.axis_index("row"), lax.div(lax.axis_index("col"), n_x), n_z // 2
    places = []
    for m in range(sums.shape[0]):
        wanted = z ^ (2 * m if z_first else m)
        away = lax.rem(lax.div(row, 2) - lax.div(wanted, 2) + n_y, n_y)
        places.append(away if z_first else 2 * away + lax.rem(row + wanted, 2))
    for m in range(0, len(places), 2):
        kept_ref[m // 2] = sums[places[m]]
        code_into(sent_ref.at[m // 2], [sums[places[m + 1], ab] for ab in range(ab_tiles)])


def z_pair_kernel(parts, near_ref, near_received, far_ref, far_received, kept_ref, *send_refs):
    ab_tiles, each = kept_ref.shape[1:3]
    at = 0
    for keep_ref, received in ((near_ref, near_received), (far_ref, far_received)):
        for item in range(keep_ref.shape[0]):
            factor = tail_scales(received.at[item], ab_tiles, each)
            tiles = [add_decoded(keep_ref[item, ab], received.at[item], ab, ab_tiles, factor) for ab in range(ab_tiles)]
            part = item % parts
            if part:
                code_into(send_refs[part - 1].at[at], tiles)
            else:
                for ab in range(ab_tiles):
                    kept_ref[at, ab] = tiles[ab]
            at += part == parts - 1


def zx_pair_kernel(n_x, n_z, keep_ref, *refs):
    *received, kept_ref, sent_ref, sums = refs
    ab_tiles, each = sums.shape[1:3]
    for item in range(keep_ref.shape[0]):
        factors = [tail_scales(ref.at[item], ab_tiles, each) for ref in received]
        for ab in range(ab_tiles):
            total = keep_ref[item, ab]
            for ref, factor in zip(received, factors):
                total = add_decoded(total, ref.at[item], ab, ab_tiles, factor)
            sums[item, ab] = total
    put_in_order(True, n_x, n_z, sums, kept_ref, sent_ref)


def halve_kernel(kept_ref, received_ref, next_ref, sent_ref):
    count, ab_tiles, each, width = kept_ref.shape
    for item in range(count):
        factor = tail_scales(received_ref.at[item], ab_tiles, each)
        tiles = [
            add_decoded(kept_ref[item, ab], received_ref.at[item], ab, ab_tiles, factor) for ab in range(ab_tiles)
        ]
        if item % 2:
            code_into(sent_ref.at[item // 2], tiles)
        else:
            for ab in range(ab_tiles):
                next_ref[item // 2, ab] = tiles[ab]


def last_kernel(*refs):
    flat, out_ref = refs[-1], refs[-2]
    rows, ab_tiles, width = out_ref.shape
    lanes = flat.shape[2]
    start = 0
    for kept_ref, received_ref in zip(refs[:-2:2], refs[1:-2:2]):
        each = kept_ref.shape[2]
        factor = tail_scales(received_ref.at[0], ab_tiles, each)
        for ab in range(ab_tiles):
            total = add_decoded(kept_ref[0, ab], received_ref.at[0], ab, ab_tiles, factor)
            for half in range(width // lanes):
                piece = total[:, half * lanes : (half + 1) * lanes]
                flat[half, pl.ds(start * ab_tiles + ab, each, stride=ab_tiles), :] = piece
        start += each
    for half in range(width // lanes):
        whole = flat[half].reshape(rows, ab_tiles, lanes)
        out_ref[:, :, pl.ds(half * lanes, lanes)] = whole.astype(out_ref.dtype)


def shards(n_row, n_col, amps, ints, task_cd, task_ab, task_count):
    n_x = n_col // n_row
    n_z = n_row
    n_y = n_row // 2
    rows, tiles, width = amps.shape
    out_rows = rows // n_x
    sizes = [out_rows // 2] * 2
    pairs = PAIR_TILES_ROW * CD_COL
    other_parts = range(1, n_x)

    def along_y(array, step):
        return lax.ppermute(array, "row", [(r, (r + 2 * step) % n_row) for r in range(n_row)])

    def to_partner(array):
        return lax.ppermute(array, "row", [(r, r ^ 1) for r in range(n_row)])

    def along_x(array, step):
        pairs = [(c, c - c % n_x + (c % n_x + step) % n_x) for c in range(n_col)]
        return lax.ppermute(array, "col", pairs)

    def along_z(array, bit):
        return lax.ppermute(array, "col", [(c, (c // n_x ^ bit) * n_x + c % n_x) for c in range(n_col)])

    def coded(each, *lead):
        return pltpu.VMEM((*lead, PAIR_TILES_ROW * each + 16, width), I16)

    def summed(each, *lead):
        return pltpu.VMEM((*lead, PAIR_TILES_ROW, each, width), F32)

    hbm = functools.partial(pltpu.with_memory_space_constraint, memory_space=pltpu.HBM)

    def products(blocks, x_first):
        count, each = len(blocks), blocks[0].shape[2]
        if x_first:
            outs = [summed(each, count)] + [coded(each, count)] * (n_x - 1)
        else:
            outs = [summed(each, count * n_x // 2), coded(each, count * n_x // 2)]
        return kernel_call(
            functools.partial(product_kernel, count, x_first),
            outs,
            [IN_VMEM] * count + [IN_SMEM, IN_VMEM],
            [pltpu.VMEM((tiles + 1, count * n_x * each, width), BF16)],
            name="x_products" if x_first else "z_products",
        )(*map(held, blocks), slots, held(table))

    mine = kernel_call(
        functools.partial(split_kernel, n_x),
        [pltpu.VMEM((n_x, tiles, each, width), BF16) for each in sizes],
        [IN_HBM],
        [
            pltpu.VMEM(amps.shape, BF16),
            pltpu.VMEM((width // LANES, rows * tiles, LANES), F32),
            pltpu.SemaphoreType.DMA,
        ],
        name="split",
    )(hbm(amps))
    far = [[along_y(chunk, k) for k in range(1, n_y)] for chunk in mine]
    beside = [to_partner(chunk) for chunk in mine]
    slots, table = kernel_call(
        functools.partial(load_kernel, LOADS),
        [pltpu.SMEM((2 * pairs,), jnp.int32), pltpu.VMEM(ints.shape, BF16)],
        [IN_SMEM] + [IN_HBM] * 3,
        [
            pltpu.SMEM(task_cd.shape, jnp.int32),
            pltpu.SMEM(task_ab.shape, jnp.int32),
            pltpu.SemaphoreType.DMA((2 + LOADS,)),
        ],
        outputs=[IN_SMEM, IN_VMEM],
        name="load",
    )(task_count, hbm(task_cd), hbm(task_ab), hbm(ints))

    def over_x(sends):
        return [along_x(send, step) for step, send in zip(range(1, n_x), sends)]

    def fetch(arrays, *ties):
        blocks = []
        for array in arrays:
            array = after(array, *ties)
            blocks += [array, to_partner(array)]
        return blocks

    def reduce_z(kept, sent, bit):
        each, count = kept.shape[2], kept.shape[0]
        received = along_z(sent, bit)
        while count > 1:
            count, bit = count // 2, bit * 2
            kept, sent = kernel_call(
                halve_kernel, [summed(each, count), coded(each, count)], [IN_VMEM] * 2, name="halve"
            )(held(kept), held(received))
            received = along_z(sent, bit)
        return [kept, received]

    near_keep, *sends = products([mine[0], beside[0]], True)
    near_received = over_x(sends)
    near_zkeep, send = products([after(mine[1], near_keep), beside[1]], False)
    near_zreceived = along_z(send, 1)
    far_blocks = fetch(far[0], near_zkeep)
    far_keep, *sends = products(far_blocks, True)
    far_received = over_x(sends)
    far_zblocks = fetch(far[1], far_keep)
    far_zkeep, send = products([after(v, near_received[-1], near_zreceived) for v in far_zblocks], False)
    far_zreceived = along_z(send, 1)

    first, second = sizes
    kept, sent = kernel_call(
        functools.partial(x_pair_kernel, n_x, n_z),
        [summed(first, n_z // 2), coded(first, n_z // 2)],
        [IN_VMEM] * (2 * n_x),
        [summed(first, n_z)],
        name="x_pairs",
        hint=HINT,
    )(*map(held, [near_keep, *near_received, far_keep, *far_received]))
    last = reduce_z(kept, sent, 1)
    kept, *sends = kernel_call(
        functools.partial(z_pair_kernel, n_x),
        [summed(second, n_y)] + [coded(second, n_y)] * (n_x - 1),
        [IN_VMEM] * 4,
        name="z_pairs",
    )(*map(held, [near_zkeep, near_zreceived, far_zkeep, far_zreceived]))
    kept, sent = kernel_call(
        functools.partial(zx_pair_kernel, n_x, n_z),
        [summed(second, n_y // 2), coded(second, n_y // 2)],
        [IN_VMEM] * n_x,
        [summed(second, n_y)],
        name="zx_pairs",
    )(*map(held, [kept, *over_x(sends)]))
    last += reduce_z(kept, sent, 2)
    return kernel_call(
        last_kernel,
        jax.ShapeDtypeStruct((out_rows, PAIR_TILES_ROW, width), BF16),
        [IN_VMEM] * len(last),
        [pltpu.VMEM((width // LANES, out_rows * PAIR_TILES_ROW, LANES), F32)],
        name="last",
    )(*map(held, last))


def solution(mesh):
    return jax.shard_map(
        functools.partial(shards, mesh.shape["row"], mesh.shape["col"]),
        mesh=mesh,
        in_specs=(
            P("row", "col", None),
            P(("row", "col"), None, None),
            P(("row", "col")),
            P(("row", "col")),
            P(("row", "col")),
        ),
        out_specs=P("col", "row", None),
        check_vma=False,
    )
```

```python
import functools

import jax
import jax.numpy as jnp
from jax import lax
from jax.experimental import pallas as pl
from jax.experimental.pallas import tpu as pltpu
from jax.sharding import PartitionSpec as P

CD_COL = 8
PAIR_TILES_ROW = 8
LOADS = 8
HINT = 3 * 10**9
LANES = 128
LEVELS = 32000.0
STEPS = 64.0
SMALLEST = 2.0**-110
VMEM_LIMIT = 16 * 1024 * 1024

F32 = jnp.float32
BF16 = jnp.bfloat16
I16 = jnp.int16

IN_VMEM = pl.BlockSpec(memory_space=pltpu.VMEM)
IN_SMEM = pl.BlockSpec(memory_space=pltpu.SMEM)
IN_HBM = pl.BlockSpec(memory_space=pl.ANY)


def held(x):
    return pltpu.with_memory_space_constraint(x, pltpu.VMEM)


def after(x, *others):
    return lax.optimization_barrier((x, *others))[0]


def kernel_call(body, outs, ins, scratch=(), name=None, hint=0, outputs=IN_VMEM):
    return pl.pallas_call(
        body,
        out_shape=outs,
        in_specs=ins,
        out_specs=outputs if outputs is not IN_VMEM else jax.tree.map(lambda _: IN_VMEM, outs),
        scratch_shapes=list(scratch),
        compiler_params=pltpu.CompilerParams(vmem_limit_bytes=VMEM_LIMIT),
        cost_estimate=pl.CostEstimate(flops=1 + hint, bytes_accessed=1, transcendentals=0),
        name=name,
    )


def code(block):
    top = jnp.maximum(jnp.max(jnp.abs(block), axis=0, keepdims=True), SMALLEST)
    exponent = jnp.ceil(jnp.log2(top) * STEPS)
    scaled = block * (LEVELS * jnp.exp2(exponent * (-1.0 / STEPS)))
    return jnp.round(scaled).astype(jnp.int32).astype(I16), exponent


def store_exponents(ref, rows):
    pad = -len(rows) % 16
    block = jnp.concatenate(list(rows) + [jnp.zeros_like(rows[0])] * pad, axis=0)
    ref[ref.shape[0] - len(rows) - pad :] = block.astype(jnp.int32).astype(I16)


def scales(exponents):
    return jnp.exp2(exponents.astype(jnp.int32).astype(F32) * (1.0 / STEPS)) * (1.0 / LEVELS)


def decode(block, scale):
    return block.astype(jnp.int32).astype(F32) * scale


def split_kernel(parts, amps_hbm, *refs):
    outs, (amps, flat, sem) = refs[:-3], refs[-3:]
    rows, tiles, width = amps.shape
    lanes = flat.shape[2]
    copy = pltpu.make_async_copy(amps_hbm, amps, sem)
    copy.start()
    copy.wait()
    for half in range(width // lanes):
        columns = pl.ds(half * lanes, lanes)
        flat[half] = amps[:, :, columns].astype(F32).reshape(rows * tiles, lanes)
    here = lax.rem(lax.axis_index("col"), parts)
    start = 0
    for out in outs:
        each = out.shape[2]
        for step in range(parts):
            part = lax.rem(here + step, parts)
            for tile in range(tiles):
                first = (part * (rows // parts) + start) * tiles + tile
                for half in range(width // lanes):
                    picked = flat[half, pl.ds(first, each, stride=tiles), :]
                    out[step, tile, :, pl.ds(half * lanes, lanes)] = picked.astype(BF16)
        start += each


def load_kernel(pieces, count_ref, cd_hbm, ab_hbm, ints_hbm, slots_ref, table_ref, cd, ab, sems):
    per = ints_hbm.shape[0] // pieces
    pairs = slots_ref.shape[0] // 2
    copies = [pltpu.make_async_copy(cd_hbm, cd, sems.at[0]), pltpu.make_async_copy(ab_hbm, ab, sems.at[1])]
    for piece in range(pieces):
        part = pl.ds(piece * per, per)
        copies.append(pltpu.make_async_copy(ints_hbm.at[part], table_ref.at[part], sems.at[2 + piece]))
    for copy in copies:
        copy.start()

    def clear(pair, carry):
        slots_ref[pair] = 0
        slots_ref[pairs + pair] = CD_COL
        return carry

    def note(slot, carry):
        pair = ab[slot] * CD_COL + cd[slot]
        slots_ref[pair] = slot
        slots_ref[pairs + pair] = cd[slot]
        return carry

    lax.fori_loop(0, pairs, clear, 0)
    copies[0].wait()
    copies[1].wait()
    lax.fori_loop(0, count_ref[0], note, 0)
    for copy in copies[2:]:
        copy.wait()


def multiply(left, slots_ref, table_ref, use):
    tiles, rows = left.shape[0] - 1, left.shape[1]
    pairs = slots_ref.shape[0] // 2
    left[tiles] = jnp.zeros(left.shape[1:], BF16)
    for ab in range(pairs // tiles):
        total = jnp.zeros((rows, table_ref.shape[2]), F32)
        for tile in range(tiles):
            pair = ab * tiles + tile
            total = total + jnp.dot(
                left[slots_ref[pairs + pair]], table_ref[slots_ref[pair]], preferred_element_type=F32
            )
        use(ab, total)


def product_kernel(blocks, x_first, *refs):
    amps_refs, (slots_ref, table_ref) = refs[:blocks], refs[blocks : blocks + 2]
    keep_ref, send_refs, left = refs[blocks + 2], refs[blocks + 3 : -1], refs[-1]
    parts, tiles, each, _ = amps_refs[0].shape
    kept = keep_ref.shape[0]
    if x_first:
        order = [(block, part) for part in range(parts) for block in range(blocks)]
        for tile in range(tiles):
            for at, (block, part) in enumerate(order):
                left[tile, at * each : (at + 1) * each] = amps_refs[block][part, tile]
    else:
        swapped = lax.rem(lax.axis_index("row") + lax.div(lax.axis_index("col"), parts), 2) == 1
        for tile in range(tiles):
            for pair in range(blocks // 2):
                for part in range(parts):
                    even, odd = amps_refs[2 * pair][part, tile], amps_refs[2 * pair + 1][part, tile]
                    at = pair * parts + part
                    left[tile, at * each : (at + 1) * each] = jnp.where(swapped, odd, even)
                    at += kept
                    left[tile, at * each : (at + 1) * each] = jnp.where(swapped, even, odd)
    sends = [(ref, item) for ref in send_refs for item in range(kept)]
    ab_tiles = slots_ref.shape[0] // 2 // tiles
    exponents = [[] for _ in sends]

    def use(ab, total):
        for at in range(kept):
            keep_ref[at, ab] = total[at * each : (at + 1) * each]
        for at, (ref, item) in enumerate(sends):
            first = (kept + at) * each
            coded, exponent = code(total[first : first + each])
            to = (item * ab_tiles + ab) * each
            ref[to : to + each] = coded
            exponents[at].append(exponent)

    multiply(left, slots_ref, table_ref, use)
    for at, ref in enumerate(send_refs):
        store_exponents(ref, sum(exponents[at * kept : (at + 1) * kept], []))


def add_decoded(total, ref, at, factors):
    each = total.shape[0]
    return total + decode(ref[at * each : (at + 1) * each], factors[at : at + 1])


def tail_scales(ref, blocks, each):
    return scales(ref[blocks * each :])


def code_into(ref, item, tiles):
    each = tiles[0].shape[0]
    exponents = []
    for ab, tile in enumerate(tiles):
        coded, exponent = code(tile)
        at = (item * len(tiles) + ab) * each
        ref[at : at + each] = coded
        exponents.append(exponent)
    return exponents


def x_pair_kernel(n_x, n_z, *refs):
    refs, (kept_ref, sent_ref, sums) = refs[:-3], refs[-3:]
    half = len(refs) // 2
    ab_tiles, each = sums.shape[1:3]
    at = 0
    for keep_ref, *received in (refs[:half], refs[half:]):
        factors = [tail_scales(ref, keep_ref.shape[0] * ab_tiles, each) for ref in received]
        for item in range(keep_ref.shape[0]):
            for ab in range(ab_tiles):
                total = keep_ref[item, ab]
                for ref, factor in zip(received, factors):
                    total = add_decoded(total, ref, item * ab_tiles + ab, factor)
                sums[at, ab] = total
            at += 1
    put_in_order(False, n_x, n_z, sums, kept_ref, sent_ref)


def put_in_order(z_first, n_x, n_z, sums, kept_ref, sent_ref):
    ab_tiles = sums.shape[1]
    row, z, n_y = lax.axis_index("row"), lax.div(lax.axis_index("col"), n_x), n_z // 2
    places = []
    for m in range(sums.shape[0]):
        wanted = z ^ (2 * m if z_first else m)
        away = lax.rem(lax.div(row, 2) - lax.div(wanted, 2) + n_y, n_y)
        places.append(away if z_first else 2 * away + lax.rem(row + wanted, 2))
    exponents = []
    for m in range(0, len(places), 2):
        kept_ref[m // 2] = sums[places[m]]
        exponents += code_into(sent_ref, m // 2, [sums[places[m + 1], ab] for ab in range(ab_tiles)])
    store_exponents(sent_ref, exponents)


def z_pair_kernel(parts, near_ref, near_received, far_ref, far_received, kept_ref, *send_refs):
    ab_tiles, each = kept_ref.shape[1:3]
    at = 0
    exponents = [[] for _ in send_refs]
    for keep_ref, received in ((near_ref, near_received), (far_ref, far_received)):
        factor = tail_scales(received, keep_ref.shape[0] * ab_tiles, each)
        for item in range(keep_ref.shape[0]):
            tiles = [
                add_decoded(keep_ref[item, ab], received, item * ab_tiles + ab, factor) for ab in range(ab_tiles)
            ]
            part = item % parts
            if part:
                exponents[part - 1] += code_into(send_refs[part - 1], at, tiles)
            else:
                for ab in range(ab_tiles):
                    kept_ref[at, ab] = tiles[ab]
            at += part == parts - 1
    for ref, rows in zip(send_refs, exponents):
        store_exponents(ref, rows)


def zx_pair_kernel(n_x, n_z, keep_ref, *refs):
    *received, kept_ref, sent_ref, sums = refs
    ab_tiles, each = sums.shape[1:3]
    factors = [tail_scales(ref, keep_ref.shape[0] * ab_tiles, each) for ref in received]
    for item in range(keep_ref.shape[0]):
        for ab in range(ab_tiles):
            total = keep_ref[item, ab]
            for ref, factor in zip(received, factors):
                total = add_decoded(total, ref, item * ab_tiles + ab, factor)
            sums[item, ab] = total
    put_in_order(True, n_x, n_z, sums, kept_ref, sent_ref)


def halve_kernel(kept_ref, received_ref, next_ref, sent_ref):
    count, ab_tiles, each, _ = kept_ref.shape
    factor = tail_scales(received_ref, count * ab_tiles, each)
    exponents = []
    for item in range(count):
        tiles = [
            add_decoded(kept_ref[item, ab], received_ref, item * ab_tiles + ab, factor) for ab in range(ab_tiles)
        ]
        if item % 2:
            exponents += code_into(sent_ref, item // 2, tiles)
        else:
            for ab in range(ab_tiles):
                next_ref[item // 2, ab] = tiles[ab]
    store_exponents(sent_ref, exponents)


def last_kernel(*refs):
    *ready_refs, kept_ref, received_ref, out_ref, flat = refs
    each, ab_tiles, lanes = kept_ref.shape[2], out_ref.shape[1], flat.shape[2]
    start = 0
    for ready_ref in ready_refs:
        out_ref[start : start + ready_ref.shape[0]] = ready_ref[...]
        start += ready_ref.shape[0]
    factor = tail_scales(received_ref, ab_tiles, each)
    for ab in range(ab_tiles):
        total = add_decoded(kept_ref[0, ab], received_ref, ab, factor)
        for half in range(out_ref.shape[2] // lanes):
            flat[half, pl.ds(ab, each, stride=ab_tiles), :] = total[:, half * lanes : (half + 1) * lanes]
    for half in range(out_ref.shape[2] // lanes):
        whole = flat[half].reshape(each, ab_tiles, lanes)
        out_ref[start : start + each, :, pl.ds(half * lanes, lanes)] = whole.astype(out_ref.dtype)


def shards(n_row, n_col, amps, ints, task_cd, task_ab, task_count):
    n_x = n_col // n_row
    n_z = n_row
    n_y = n_row // 2
    rows, tiles, width = amps.shape
    out_rows = rows // n_x
    sizes = [out_rows // 2] * 2
    pairs = PAIR_TILES_ROW * CD_COL
    other_parts = range(1, n_x)

    def along_y(array, step):
        return lax.ppermute(array, "row", [(r, (r + 2 * step) % n_row) for r in range(n_row)])

    def to_partner(array):
        return lax.ppermute(array, "row", [(r, r ^ 1) for r in range(n_row)])

    def along_x(array, step):
        pairs = [(c, c - c % n_x + (c % n_x + step) % n_x) for c in range(n_col)]
        return lax.ppermute(array, "col", pairs)

    def along_z(array, bit):
        return lax.ppermute(array, "col", [(c, (c // n_x ^ bit) * n_x + c % n_x) for c in range(n_col)])

    def coded(each, count):
        blocks = count * PAIR_TILES_ROW
        return pltpu.VMEM((blocks * each + -(-blocks // 16) * 16, width), I16)

    def summed(each, *lead):
        return pltpu.VMEM((*lead, PAIR_TILES_ROW, each, width), F32)

    hbm = functools.partial(pltpu.with_memory_space_constraint, memory_space=pltpu.HBM)

    def products(blocks, x_first):
        count, each = len(blocks), blocks[0].shape[2]
        if x_first:
            outs = [summed(each, count)] + [coded(each, count)] * (n_x - 1)
        else:
            outs = [summed(each, count * n_x // 2), coded(each, count * n_x // 2)]
        return kernel_call(
            functools.partial(product_kernel, count, x_first),
            outs,
            [IN_VMEM] * count + [IN_SMEM, IN_VMEM],
            [pltpu.VMEM((tiles + 1, count * n_x * each, width), BF16)],
            name="x_products" if x_first else "z_products",
        )(*map(held, blocks), slots, held(table))

    mine = kernel_call(
        functools.partial(split_kernel, n_x),
        [pltpu.VMEM((n_x, tiles, each, width), BF16) for each in sizes],
        [IN_HBM],
        [
            pltpu.VMEM(amps.shape, BF16),
            pltpu.VMEM((width // LANES, rows * tiles, LANES), F32),
            pltpu.SemaphoreType.DMA,
        ],
        name="split",
    )(hbm(amps))
    far = [[along_y(chunk, k) for k in range(1, n_y)] for chunk in mine]
    beside = [to_partner(chunk) for chunk in mine]
    slots, table = kernel_call(
        functools.partial(load_kernel, LOADS),
        [pltpu.SMEM((2 * pairs,), jnp.int32), pltpu.VMEM(ints.shape, BF16)],
        [IN_SMEM] + [IN_HBM] * 3,
        [
            pltpu.SMEM(task_cd.shape, jnp.int32),
            pltpu.SMEM(task_ab.shape, jnp.int32),
            pltpu.SemaphoreType.DMA((2 + LOADS,)),
        ],
        outputs=[IN_SMEM, IN_VMEM],
        name="load",
    )(task_count, hbm(task_cd), hbm(task_ab), hbm(ints))

    def over_x(sends):
        return [along_x(send, step) for step, send in zip(range(1, n_x), sends)]

    def fetch(arrays, *ties):
        blocks = []
        for array in arrays:
            array = after(array, *ties)
            blocks += [array, to_partner(array)]
        return blocks

    def reduce_z(kept, sent, bit):
        each, count = kept.shape[2], kept.shape[0]
        received = along_z(sent, bit)
        while count > 1:
            count, bit = count // 2, bit * 2
            kept, sent = kernel_call(
                halve_kernel, [summed(each, count), coded(each, count)], [IN_VMEM] * 2, name="halve"
            )(held(kept), held(received))
            received = along_z(sent, bit)
        return [kept, received]

    def finish(place, kept, received, *ready):
        each = kept.shape[2]
        return kernel_call(
            last_kernel,
            place((each + sum(v.shape[0] for v in ready), PAIR_TILES_ROW, width), BF16),
            [IN_VMEM] * (len(ready) + 2),
            [pltpu.VMEM((width // LANES, each * PAIR_TILES_ROW, LANES), F32)],
            name="last",
        )(*ready, held(kept), held(received))

    near_keep, *sends = products([mine[0], beside[0]], True)
    near_received = over_x(sends)
    near_zkeep, send = products([after(mine[1], near_keep), beside[1]], False)
    near_zreceived = along_z(send, 1)
    far_blocks = fetch(far[0], near_zkeep)
    far_keep, *sends = products(far_blocks, True)
    far_received = over_x(sends)
    far_zblocks = fetch(far[1], far_keep)
    far_zkeep, send = products([after(v, near_received[-1], near_zreceived) for v in far_zblocks], False)
    far_zreceived = along_z(send, 1)

    first, second = sizes
    kept, sent = kernel_call(
        functools.partial(x_pair_kernel, n_x, n_z),
        [summed(first, n_z // 2), coded(first, n_z // 2)],
        [IN_VMEM] * (2 * n_x),
        [summed(first, n_z)],
        name="x_pairs",
        hint=HINT,
    )(*map(held, [near_keep, *near_received, far_keep, *far_received]))
    ready = finish(pltpu.VMEM, *reduce_z(kept, sent, 1))
    kept, *sends = kernel_call(
        functools.partial(z_pair_kernel, n_x),
        [summed(second, n_y)] + [coded(second, n_y)] * (n_x - 1),
        [IN_VMEM] * 4,
        name="z_pairs",
    )(*map(held, [near_zkeep, near_zreceived, far_zkeep, far_zreceived]))
    kept, sent = kernel_call(
        functools.partial(zx_pair_kernel, n_x, n_z),
        [summed(second, n_y // 2), coded(second, n_y // 2)],
        [IN_VMEM] * n_x,
        [summed(second, n_y)],
        name="zx_pairs",
    )(*map(held, [kept, *over_x(sends)]))
    return finish(jax.ShapeDtypeStruct, *reduce_z(kept, sent, 2), held(ready))


def solution(mesh):
    return jax.shard_map(
        functools.partial(shards, mesh.shape["row"], mesh.shape["col"]),
        mesh=mesh,
        in_specs=(
            P("row", "col", None),
            P(("row", "col"), None, None),
            P(("row", "col")),
            P(("row", "col")),
            P(("row", "col")),
        ),
        out_specs=P("col", "row", None),
        check_vma=False,
    )
```
